32 devices in a mesh: phase: 2 (over x), ctx: 4 (over z), head: 4 (over y, core).
Axes of the slice: x: 2, y: 2, z: 4, core: 2. Of those that a mesh axis runs over, the one named last changes fastest.
Arguments:
- query: bfloat16 [2, 1024, 5120], P('phase', 'ctx', 'head'), may hold values from -18 to 18
- key_cache: bfloat16 [1024, 1024], P('ctx', 'head'), may hold values from -18 to 18
- value_cache: bfloat16 [1024, 1024], P('ctx', 'head'), may hold values from -6 to 6
- saved_output: bfloat16 [2, 1024, 5120], P('phase', 'ctx', 'head'), may hold values from -1.796875 to 1.796875
- out_grad: bfloat16 [2, 1024, 5120], P('phase', 'ctx', 'head'), may hold values from -6 to 6
- out_weight: bfloat16 [2, 5120, 5120], P('phase', 'head'), may hold values from -0.078125 to 0.078125
- doc_lengths: int32 [4], replicated, may hold values from 1 to 768, 1024 in all
Outputs:
- grad_query: float32 [2, 1024, 5120], P('phase', 'ctx', 'head')
- grad_key: float32 [1024, 1024], P('ctx', 'head')
- grad_value: float32 [1024, 1024], P('ctx', 'head')
The draws below stay inside these ranges and needn't reach their ends.
Inputs may be any that keep to these rules, and one draw needn't show every extreme that they name: `doc_lengths`: the 4 lengths sum to 1024, and one document has exactly 768 positions.
All inputs are finite; a program needn't handle non-finite values.
Results may differ from the reference program's by a relative error of at most 0.0041.
Values may be sent and summed in bfloat16 or wider, within the bound.
A program may use at most 128 MiB of HBM per device.

```python
import math
import jax
import jax.numpy as jnp
import numpy as np
from jax import lax

D = 5120
HQ = 40
KVH = 8
HD = 128
BLOCK = 512
DOCS = 4
SECTIONS = 2
LEN = 1024
DOC_MOST = 768


def paired_draw(key):
    base = jax.random.fold_in(key, 7001)
    groups = HQ // KVH
    key_rows = jax.random.normal(jax.random.fold_in(base, 1), (LEN, KVH, HD), jnp.float32)
    query_rows = jax.random.normal(jax.random.fold_in(base, 2), (SECTIONS, LEN, KVH, groups, HD), jnp.float32)
    key_rows = jnp.clip(key_rows, -6.0, 6.0)
    query_rows = jnp.clip(query_rows, -6.0, 6.0)
    return (query_rows.reshape(SECTIONS, LEN, HQ * HD), key_rows.reshape(LEN, KVH * HD))


def draw_query(key, part):
    return paired_draw(key)[0].astype(jnp.bfloat16)


def draw_key_cache(key, part):
    return paired_draw(key)[1].astype(jnp.bfloat16)


def steps_of(rng, dims, shards, low, top_value):
    factor_of = 1.0
    for axis_at, shards_of in shards:
        draws = jax.random.uniform(jax.random.fold_in(jax.random.fold_in(rng, 6), axis_at), (shards_of,), jnp.float32, low / len(shards), top_value / len(shards))
        factor_of = factor_of * jnp.repeat(jnp.exp(draws), dims[axis_at] // shards_of).reshape((-1,) + (1,) * (len(dims) - 1 - axis_at))
    return factor_of


def profile(count, total, bound, lean):
    portions = [(1 << 20) // math.isqrt(standing ** lean) + 1 for standing in range(2, count + 1)]
    rest, holding = total - bound - (count - 1), [1] * (count - 1)
    while rest > 0:
        candidates = [i for i in range(count - 1) if holding[i] < bound]
        whole, remaining = sum([portions[i] for i in candidates]), rest
        for i in candidates:
            addition = min(bound - holding[i], max(1, remaining * portions[i] // whole), rest)
            holding[i] = holding[i] + addition
            rest = rest - addition
    return np.array([bound] + holding)


def uneven_parts(rng, amount, total, limit, lean):
    if amount == 2:
        one = jax.random.randint(rng, (), max(1, total - limit), min(limit, total - 1) + 1)
        return jnp.stack([one, total - one])
    lengths = jnp.asarray(profile(amount, total, limit, lean), jnp.int32)
    couples = (amount - 1) // 2
    source_of, sink = lengths[1:1 + 2 * couples:2], lengths[2:2 + 2 * couples:2]
    slack = jnp.minimum(source_of - 1, limit - sink)
    passed = jax.random.randint(jax.random.fold_in(rng, 1), (couples,), 0, 1 << 20) % (slack + 1)
    lengths = lengths.at[1:1 + 2 * couples:2].set(source_of - passed).at[2:2 + 2 * couples:2].set(sink + passed)
    return lengths[jax.random.permutation(jax.random.fold_in(rng, 2), amount)]


def scatter_about(stream_key, extent, scale, reach, pieces=(), kind=jnp.bfloat16):
    gain = steps_of(stream_key, extent, pieces, -0.22, 0.18) if pieces else 1.0
    array = jax.random.normal(stream_key, extent, jnp.float32) * scale * gain
    return jnp.minimum(jnp.maximum(array, -reach), reach).astype(kind)


def setup_inputs(seed: int = 0) -> dict:
    key_list = jax.random.split(jax.random.key(seed), 8)
    return {
        "query": draw_query(jax.random.fold_in(key_list[7], 71), 0),
        "key_cache": draw_key_cache(jax.random.fold_in(key_list[7], 71), 0),
        "value_cache": scatter_about(key_list[2], (LEN, KVH * HD), 1.0, 6.0, ((0, 4), (1, 4))),
        "saved_output": scatter_about(key_list[3], (SECTIONS, LEN, HQ * HD), 0.3, 1.796875, ((0, 2), (1, 4), (2, 4))),
        "out_grad": scatter_about(key_list[4], (SECTIONS, LEN, D), 1.0, 6.0, ((0, 2), (1, 4), (2, 4))),
        "out_weight": scatter_about(key_list[5], (SECTIONS, D, HQ * HD), D ** -0.5, 0.078125, ((0, 2), (1, 4))),
        "doc_lengths": uneven_parts(key_list[6], DOCS, LEN, DOC_MOST, 2).astype(jnp.int32),
    }


MASKED = -1.0e30


def reference(query, key_cache, value_cache, saved_output, out_grad, out_weight, doc_lengths):
    scale = HD ** -0.5
    groups = HQ // KVH
    places = jnp.arange(LEN, dtype=jnp.int32)
    ends = jnp.cumsum(doc_lengths).astype(jnp.int32)
    segment = jnp.sum((places[:, None] >= ends[None, :]).astype(jnp.int32), axis=1)

    def project(index):
        return jnp.dot(out_grad[index], out_weight[index], preferred_element_type=jnp.float32).astype(jnp.bfloat16)

    grad_attn = lax.map(project, jnp.arange(SECTIONS, dtype=jnp.int32))
    query_heads = query.reshape(SECTIONS, LEN, KVH, groups, HD)
    grad_heads = grad_attn.reshape(SECTIONS, LEN, KVH, groups, HD)
    output_heads = saved_output.reshape(SECTIONS, LEN, KVH, groups, HD)
    key_heads = key_cache.reshape(LEN, KVH, HD)
    value_heads = value_cache.reshape(LEN, KVH, HD)
    blocks = LEN // BLOCK

    def one_head(index):
        section = index // KVH
        head_index = index % KVH
        query_one = query_heads[section, :, head_index].astype(jnp.float32)
        grad_one = grad_heads[section, :, head_index].astype(jnp.float32)
        output_one = output_heads[section, :, head_index].astype(jnp.float32)
        key_one = key_heads[:, head_index].astype(jnp.float32)
        value_one = value_heads[:, head_index].astype(jnp.float32)
        delta = jnp.sum(grad_one * output_one, axis=-1)

        def one_block(carry, block_index):
            start = (block_index * BLOCK).astype(jnp.int32)
            query_block = lax.dynamic_slice_in_dim(query_one, start, BLOCK, 0)
            grad_block = lax.dynamic_slice_in_dim(grad_one, start, BLOCK, 0)
            delta_block = jnp.transpose(lax.dynamic_slice_in_dim(delta, start, BLOCK, 0))
            query_place = lax.dynamic_slice_in_dim(places, start, BLOCK, 0)
            query_segment = lax.dynamic_slice_in_dim(segment, start, BLOCK, 0)
            allowed = (places[None, :] <= query_place[:, None]) & (segment[None, :] == query_segment[:, None])
            scores = jnp.einsum("tgd,kd->gtk", query_block, key_one) * scale
            scores = jnp.where(allowed[None], scores, MASKED)
            largest = jnp.max(scores, axis=-1, keepdims=True)
            total = jnp.sum(jnp.where(allowed[None], jnp.exp(scores - largest), 0.0), axis=-1, keepdims=True)
            log_total = largest + jnp.log(total)
            weights = jnp.where(allowed[None], jnp.exp(scores - log_total), 0.0)
            weights_low = lax.optimization_barrier(weights.astype(jnp.bfloat16)).astype(jnp.float32)
            value_grad = jnp.einsum("gtk,tgd->kd", weights_low, grad_block)
            weight_grad = jnp.einsum("tgd,kd->gtk", grad_block, value_one)
            score_grad = (weights * (weight_grad - delta_block[:, :, None])).astype(jnp.bfloat16)
            score_grad = lax.optimization_barrier(score_grad).astype(jnp.float32)
            query_grad = jnp.einsum("gtk,kd->tgd", score_grad, key_one) * scale
            key_grad = jnp.einsum("gtk,tgd->kd", score_grad, query_block) * scale
            return (carry[0] + key_grad, carry[1] + value_grad), query_grad

        zeros = jnp.zeros((LEN, HD), jnp.float32)
        (key_grad, value_grad), query_grad = lax.scan(one_block, (zeros, zeros), jnp.arange(blocks, dtype=jnp.int32))
        return query_grad.reshape(LEN, groups, HD), key_grad, value_grad

    query_all, key_all, value_all = lax.map(one_head, jnp.arange(SECTIONS * KVH, dtype=jnp.int32))
    grad_query = jnp.transpose(query_all.reshape(SECTIONS, KVH, LEN, groups, HD), (0, 2, 1, 3, 4)).reshape(SECTIONS, LEN, HQ * HD)
    grad_key = jnp.transpose(jnp.sum(key_all.reshape(SECTIONS, KVH, LEN, HD), axis=0), (1, 0, 2)).reshape(LEN, KVH * HD)
    grad_value = jnp.transpose(jnp.sum(value_all.reshape(SECTIONS, KVH, LEN, HD), axis=0), (1, 0, 2)).reshape(LEN, KVH * HD)
    return (grad_query, grad_key, grad_value)
```

```python
import jax
import jax.numpy as jnp
from jax import lax
from jax.sharding import PartitionSpec as P

HD = 128
BLOCK = 512


MASKED = -1e30


def segment_of(places, ends):
    return jnp.sum((places[:, None] >= ends[None, :]).astype(jnp.int32), axis=1)


def visible(query_place, query_segment, key_place, key_segment):
    return (key_place[None, :] <= query_place[:, None]) & (
        key_segment[None, :] == query_segment[:, None]
    )


def block_scores(queries, keys, allowed, scale):
    scores = jnp.einsum("tjgd,kjd->jgtk", queries, keys, preferred_element_type=jnp.float32) * scale
    return jnp.where(allowed[None, None], scores, MASKED)


def running_update(carry, scores, allowed):
    largest, total = carry
    raised = jnp.maximum(largest, jnp.max(scores, axis=-1))
    terms = jnp.where(allowed[None, None], jnp.exp(scores - raised[..., None]), 0.0)
    return (raised, total * jnp.exp(largest - raised) + jnp.sum(terms, axis=-1))


def block_grads(queries, grads, keys, values, allowed, log_total, delta, scale):
    scores = block_scores(queries, keys, allowed, scale)
    weights = jnp.where(allowed[None, None], jnp.exp(scores - log_total[..., None]), 0.0)
    weights_low = weights.astype(jnp.bfloat16)
    value_grad = jnp.einsum(
        "jgtk,tjgd->kjd", weights_low, grads, preferred_element_type=jnp.float32
    )
    weight_grad = jnp.einsum("tjgd,kjd->jgtk", grads, values, preferred_element_type=jnp.float32)
    score_grad = (weights * (weight_grad - delta[..., None])).astype(jnp.bfloat16)
    query_grad = jnp.einsum("jgtk,kjd->tjgd", score_grad, keys, preferred_element_type=jnp.float32)
    key_grad = jnp.einsum("jgtk,tjgd->kjd", score_grad, queries, preferred_element_type=jnp.float32)
    return (query_grad, key_grad, value_grad)


def body(query, key_cache, value_cache, saved_output, out_grad, out_weight, doc_lengths):
    rows = query.shape[1]
    query_cols = query.shape[2]
    key_cols = key_cache.shape[1]
    kv_heads = key_cols // HD
    groups = query_cols // key_cols
    scale = HD ** (-0.5)
    rank = lax.axis_index("ctx")
    documents = jnp.arange(doc_lengths.shape[0], dtype=jnp.int32)
    ends = jnp.sum(
        jnp.where(documents[None, :] <= documents[:, None], doc_lengths[None, :], 0), axis=1
    )
    query_place = rank * rows + jnp.arange(rows, dtype=jnp.int32)
    query_segment = segment_of(query_place, ends)
    grad_rows = out_grad[0]
    weight = out_weight[0]
    grad_attn = lax.psum_scatter(
        lax.dot_general(
            weight, grad_rows, (((0,), (1,)), ((), ())), preferred_element_type=jnp.float32
        ),
        "head",
        scatter_dimension=0,
        tiled=True,
    ).T.astype(jnp.bfloat16)
    queries = query[0].reshape(rows, kv_heads, groups, HD)
    grads = grad_attn.reshape(rows, kv_heads, groups, HD)
    outputs = saved_output[0].reshape(rows, kv_heads, groups, HD)
    delta = jnp.einsum("tjgd,tjgd->jgt", grads, outputs, preferred_element_type=jnp.float32)
    initial = (
        jnp.full((kv_heads, groups, rows), MASKED, jnp.float32),
        jnp.zeros((kv_heads, groups, rows), jnp.float32),
    )
    whole_keys, whole_values = (
        lax.all_gather(key_cache, "ctx", axis=0, tiled=True),
        lax.all_gather(value_cache, "ctx", axis=0, tiled=True),
    )
    length = whole_keys.shape[0]
    parts = length // BLOCK
    key_blocks = whole_keys.reshape(parts, BLOCK, kv_heads, HD)
    value_blocks = whole_values.reshape(parts, BLOCK, kv_heads, HD)
    key_places = jnp.arange(length, dtype=jnp.int32)
    key_segments = segment_of(key_places, ends).reshape(parts, BLOCK)
    key_places = key_places.reshape(parts, BLOCK)

    def stats_step(carry, inputs):
        keys, places, segments = inputs
        allowed = visible(query_place, query_segment, places, segments)
        return (running_update(carry, block_scores(queries, keys, allowed, scale), allowed), None)

    (largest, total), _ = lax.scan(stats_step, initial, (key_blocks, key_places, key_segments))
    log_total = largest + jnp.log(total)

    def grad_step(carry, inputs):
        keys, values, places, segments = inputs
        allowed = visible(query_place, query_segment, places, segments)
        query_grad, key_grad, value_grad = block_grads(
            queries, grads, keys, values, allowed, log_total, delta, scale
        )
        joined = jnp.concatenate(
            [key_grad.reshape(BLOCK, key_cols), value_grad.reshape(BLOCK, key_cols)], axis=1
        )
        return (carry + query_grad, joined)

    query_sum, kv_terms = lax.scan(
        grad_step,
        jnp.zeros((rows, kv_heads, groups, HD), jnp.float32),
        (key_blocks, value_blocks, key_places, key_segments),
    )
    mine = lax.psum_scatter(
        kv_terms.reshape(length, 2 * key_cols), "ctx", scatter_dimension=0, tiled=True
    )
    key_sum = mine[:, :key_cols] * scale
    value_sum = mine[:, key_cols:]
    query_sum = query_sum.reshape(rows, query_cols)
    key_total, value_total = lax.psum((key_sum, value_sum), "phase")
    grad_query = (query_sum * scale).reshape(1, rows, query_cols)
    return (grad_query, key_total, value_total)


def solution(mesh):
    placed = (
        P("phase", "ctx", "head"),
        P("ctx", "head"),
        P("ctx", "head"),
        P("phase", "ctx", "head"),
        P("phase", "ctx", "head"),
        P("phase", "head", None),
        P(),
    )
    return jax.shard_map(
        body,
        mesh=mesh,
        in_specs=placed,
        out_specs=(P("phase", "ctx", "head"), P("ctx", "head"), P("ctx", "head")),
        check_vma=False,
    )
```

```python
import functools
import math

import jax
import jax.numpy as jnp
from jax import lax
from jax.experimental import pallas as pl
from jax.experimental.pallas import tpu as pltpu
from jax.sharding import PartitionSpec as P

HD = 128
MASKED = -1e30
LAG = 2
MESH = pl.DeviceIdType.MESH


def nt(a, b):
    return lax.dot_general(a, b, (((1,), (1,)), ((), ())), preferred_element_type=jnp.float32)


def nn(a, b):
    return jnp.dot(a, b, preferred_element_type=jnp.float32)


def kernel(
    sizes,
    query_ref, key_ref, value_ref, saved_ref, grad_ref, weight_ref, doc_ref,
    dq_ref, dk_ref, dv_ref,
    wbuf, qbuf, obuf, kall, vall, psend, precv, ysend, yrecv, own, qs, gs, prob, bias, inv, delta,
    plow, dlow, dqt, xsend, xrecv, keep, zsend, zrecv, fsend, frecv,
    w_sem, in_sem, kv_s, kv_r, fw_s, fw_r, p_s, p_r, y_s, y_r, x_s, x_r, z_s, z_r, f_s, f_r,
):
    n, nh, rows, kvh, groups, docs, subs = sizes
    ys = nh // 2
    feats = kvh * groups * HD
    sw = feats // subs
    half = rows // 2
    scale = HD ** (-0.5)
    phase = lax.axis_index("phase")
    rank = lax.axis_index("ctx")
    head = lax.axis_index("head")
    y, core = head // 2, lax.rem(head, 2)
    other = 1 - phase
    partner = head + 1 - 2 * core
    mine = pl.ds(pl.multiple_of(phase * half, half), half)

    order = [dy for dy in range(1, ys)] + [0]
    loads = {}

    def load(dy, which, s):
        i = (dy * 2 + which) * subs + s
        dest = lax.rem(y + dy, ys) * 2 + (1 - core if which == 0 else core)
        at = pl.multiple_of(dest * feats + s * sw, HD)
        return pltpu.make_async_copy(weight_ref.at[:, pl.ds(at, sw)], wbuf.at[i], w_sem.at[i])

    def schedule():
        for dy in order:
            for t in range(subs + LAG):
                if t < subs:
                    yield dy, 0, t
                if t >= LAG:
                    yield dy, 1, t - LAG

    for step in schedule():
        loads[step] = load(*step)
        loads[step].start()
    query_copy = pltpu.make_async_copy(query_ref.at[0], qbuf, in_sem.at[0])
    saved_copy = pltpu.make_async_copy(saved_ref.at[0], obuf, in_sem.at[1])
    query_copy.start()
    saved_copy.start()

    barrier = pltpu.get_barrier_semaphore()
    pl.semaphore_signal(barrier, inc=1, device_id={"phase": other}, device_id_type=MESH)
    pl.semaphore_signal(barrier, inc=1, device_id={"head": partner}, device_id_type=MESH)
    for dy in range(1, ys):
        there = lax.rem(y + dy, ys) * 2 + core
        pl.semaphore_signal(barrier, inc=1, device_id={"head": there}, device_id_type=MESH)
    for d in range(1, n):
        pl.semaphore_signal(barrier, inc=1, device_id={"ctx": lax.rem(rank + d, n)}, device_id_type=MESH)
    pl.semaphore_wait(barrier, 2 + (ys - 1) + (n - 1))

    def kv_copy(which, d):
        src, dst = ((key_ref, kall), (value_ref, vall))[which]
        return pltpu.make_async_remote_copy(
            src_ref=src.at[mine], dst_ref=dst.at[rank, mine],
            send_sem=kv_s.at[which, d], recv_sem=kv_r.at[which, d],
            device_id={"ctx": rank + d}, device_id_type=MESH,
        )

    def kv_arrival(which, d):
        dst = (kall, vall)[which].at[rank - d, mine]
        return pltpu.make_async_remote_copy(
            src_ref=dst, dst_ref=dst,
            send_sem=fw_s.at[which, d], recv_sem=kv_r.at[which, d],
            device_id={"phase": other}, device_id_type=MESH,
        )

    def forward(which, d):
        dst = (kall, vall)[which].at[rank - d, mine]
        return pltpu.make_async_remote_copy(
            src_ref=dst, dst_ref=dst,
            send_sem=fw_s.at[which, d], recv_sem=fw_r.at[which, d],
            device_id={"phase": other}, device_id_type=MESH,
        )

    for which in range(2):
        @pl.loop(1, n - rank)
        def _(d):
            kv_copy(which, d).start()

    kall[rank] = key_ref[...]
    vall[rank] = value_ref[...]

    def to_partner(dy, s):
        i = dy * subs + s
        return pltpu.make_async_remote_copy(
            src_ref=psend.at[i], dst_ref=precv.at[i], send_sem=p_s.at[i], recv_sem=p_r.at[i],
            device_id={"head": partner}, device_id_type=MESH,
        )

    def to_chip(dy, s):
        i = (dy - 1) * subs + s
        return pltpu.make_async_remote_copy(
            src_ref=ysend.at[i], dst_ref=yrecv.at[i], send_sem=y_s.at[i], recv_sem=y_r.at[i],
            device_id={"head": lax.rem(y + dy, ys) * 2 + core}, device_id_type=MESH,
        )

    for dy, which, s in schedule():
        loads[dy, which, s].wait()
        part = nn(grad_ref[0], wbuf[(dy * 2 + which) * subs + s])
        if which == 0:
            psend[dy * subs + s] = part
            to_partner(dy, s).start()
        else:
            to_partner(dy, s).wait_recv()
            part = part + precv[dy * subs + s]
            if dy:
                ysend[(dy - 1) * subs + s] = part.astype(jnp.bfloat16)
                to_chip(dy, s).start()
            else:
                own[s] = part

    query_copy.wait()
    for j in range(kvh):
        for g in range(groups):
            qs[j, g * rows:(g + 1) * rows] = qbuf[:, (j * groups + g) * HD:(j * groups + g + 1) * HD]
    query_place = rank * rows + lax.broadcasted_iota(jnp.int32, (1, rows), 1)
    begin = jnp.zeros((1, rows), jnp.int32)
    end = jnp.int32(0)
    for d in range(docs):
        end = end + doc_ref[d]
        begin = jnp.where(query_place >= end, jnp.maximum(begin, end), begin)

    @pl.loop(0, rank + 1)
    def _(b):
        place = b * rows + lax.broadcasted_iota(jnp.int32, (rows, rows), 0)
        bias[b] = jnp.where((place <= query_place) & (place >= begin), 0.0, MASKED)

    @pl.loop(1, rank + 1)
    def _(d):
        kv_arrival(0, d).wait_recv()
        forward(0, d).start()

    @pl.loop(1, rank + 1)
    def _(d):
        kv_arrival(1, d).wait_recv()
        forward(1, d).start()

    def forwarded(which, d):
        dst = (kall, vall)[which].at[rank - d, pl.ds(pl.multiple_of(other * half, half), half)]
        return pltpu.make_async_remote_copy(
            src_ref=dst, dst_ref=dst, send_sem=fw_s.at[which, d], recv_sem=fw_r.at[which, d],
            device_id={"phase": other}, device_id_type=MESH,
        )

    @pl.loop(1, rank + 1)
    def _(d):
        forwarded(0, d).wait_recv()

    factor = scale * math.log2(math.e)
    for j in range(kvh):
        cols = slice(j * HD, (j + 1) * HD)

        def score_step(b, largest):
            raised = []
            keys = kall[b, :, cols]
            for g in range(groups):
                span = slice(g * rows, (g + 1) * rows)
                s = nt(keys, qs[j, span]) * factor + bias[b]
                prob[j, b, :, span] = s
                raised.append(jnp.maximum(largest[g], jnp.max(s, axis=0, keepdims=True)))
            return tuple(raised)

        largest = lax.fori_loop(
            0, rank + 1, score_step, (jnp.full((1, rows), MASKED, jnp.float32),) * groups
        )

        def exp_step(b, total):
            sums = []
            for g in range(groups):
                span = slice(g * rows, (g + 1) * rows)
                e = jnp.exp2(prob[j, b, :, span] - largest[g])
                prob[j, b, :, span] = e
                sums.append(total[g] + jnp.sum(e, axis=0, keepdims=True))
            return tuple(sums)

        total = lax.fori_loop(
            0, rank + 1, exp_step, (jnp.zeros((1, rows), jnp.float32),) * groups
        )
        for g in range(groups):
            inv[j, :, g * rows:(g + 1) * rows] = jnp.broadcast_to(1.0 / total[g], (8, rows))

    saved_copy.wait()
    ones = jnp.ones((8, HD), jnp.bfloat16)
    for s in range(subs):
        part = own[s]
        for dy in range(1, ys):
            to_chip(dy, s).wait_recv()
            part = part + yrecv[(dy - 1) * subs + s].astype(jnp.float32)
        low = part.astype(jnp.bfloat16)
        for at in range(0, sw, HD):
            h = (s * sw + at) // HD
            j, g = h // groups, h % groups
            span = slice(g * rows, (g + 1) * rows)
            one = low[:, at:at + HD]
            gs[j, span] = one
            both = one.astype(jnp.float32) * obuf[:, h * HD:(h + 1) * HD].astype(jnp.float32)
            high = both.astype(jnp.bfloat16)
            rest = (both - high.astype(jnp.float32)).astype(jnp.bfloat16)
            delta[j, :, span] = nt(ones, high) + nt(ones, rest)

    @pl.loop(1, rank + 1)
    def _(d):
        forwarded(1, d).wait_recv()

    def to_phase(j, b):
        return pltpu.make_async_remote_copy(
            src_ref=xsend.at[j, b], dst_ref=xrecv.at[j, b], send_sem=x_s.at[j, b], recv_sem=x_r.at[j, b],
            device_id={"phase": other}, device_id_type=MESH,
        )

    def to_owner(j, b):
        return pltpu.make_async_remote_copy(
            src_ref=zsend.at[j, b], dst_ref=zrecv.at[j, rank - b],
            send_sem=z_s.at[j, rank - b], recv_sem=z_r.at[j, rank - b],
            device_id={"ctx": b}, device_id_type=MESH,
        )

    def from_later(j, d):
        return pltpu.make_async_remote_copy(
            src_ref=zsend.at[j, 0], dst_ref=zrecv.at[j, d], send_sem=z_s.at[j, d], recv_sem=z_r.at[j, d],
            device_id={"ctx": lax.rem(rank + d, n)}, device_id_type=MESH,
        )

    def send_on(j, b):
        to_phase(j, b).wait_recv()
        zsend[j, b] = (keep[j, b] + xrecv[j, b].astype(jnp.float32)).astype(jnp.bfloat16)
        to_owner(j, b).start()

    for j in range(kvh):
        cols = slice(j * HD, (j + 1) * HD)
        dqt[...] = jnp.zeros_like(dqt)

        @pl.loop(0, rank + 1)
        def _(b):
            values = vall[b, :, cols]
            for g in range(groups):
                span = slice(g * rows, (g + 1) * rows)
                p = prob[j, b, :, span] * inv[j, 0:1, span]
                plow[:, span] = p.astype(jnp.bfloat16)
                wide = nt(values, gs[j, span])
                dlow[:, span] = (p * (wide - delta[j, 0:1, span])).astype(jnp.bfloat16)
            dv = nn(plow[...], gs[j])
            dk = nn(dlow[...], qs[j]) * scale
            keep[j, b] = jnp.where(phase == 0, dk, dv)
            xsend[j, b] = jnp.where(phase == 0, dv, dk).astype(jnp.bfloat16)
            to_phase(j, b).start()
            turned = kall[b, :, cols].astype(jnp.float32).T.astype(jnp.bfloat16)
            dqt[...] += nn(turned, dlow[...])
            if j:
                @pl.when(b < rank)
                def _():
                    send_on(j - 1, b)

        for g in range(groups):
            h = j * groups + g
            dq_ref[0, :, h * HD:(h + 1) * HD] = dqt[:, g * rows:(g + 1) * rows].T * scale

    @pl.loop(0, rank)
    def _(b):
        send_on(kvh - 1, b)

    for j in range(kvh):
        cols = slice(j * HD, (j + 1) * HD)
        to_phase(j, rank).wait_recv()
        fsend[:, cols] = keep[j, rank] + xrecv[j, rank].astype(jnp.float32)

        @pl.loop(1, n - rank)
        def _(d):
            from_later(j, d).wait_recv()
            fsend[:, cols] += zrecv[j, d].astype(jnp.float32)

    last = pltpu.make_async_remote_copy(
        src_ref=fsend, dst_ref=frecv, send_sem=f_s, recv_sem=f_r,
        device_id={"phase": other}, device_id_type=MESH,
    )
    last.start()

    for which in range(2):
        @pl.loop(1, n - rank)
        def _(d):
            kv_copy(which, d).wait_send()

        @pl.loop(1, rank + 1)
        def _(d):
            forward(which, d).wait_send()

    for dy in range(ys):
        for s in range(subs):
            to_partner(dy, s).wait_send()
            if dy:
                to_chip(dy, s).wait_send()
    for j in range(kvh):
        @pl.loop(0, rank + 1)
        def _(b):
            to_phase(j, b).wait_send()

        @pl.loop(0, rank)
        def _(b):
            to_owner(j, b).wait_send()

    last.wait()
    dk_ref[...] = jnp.where(phase == 0, fsend[...], frecv[...])
    dv_ref[...] = jnp.where(phase == 0, frecv[...], fsend[...])


def body(n, nh, query, key_cache, value_cache, saved_output, out_grad, out_weight, doc_lengths):
    rows, feats = query.shape[1:]
    width, kc = out_weight.shape[1], key_cache.shape[1]
    kvh = kc // HD
    groups = feats // kc
    ys, subs = nh // 2, groups
    sw = feats // subs
    bf, f32 = jnp.bfloat16, jnp.float32
    vmem = pltpu.VMEM
    dma = pltpu.SemaphoreType.DMA
    others = max(ys - 1, 1) * subs
    stack = groups * rows
    full = pl.BlockSpec(memory_space=pltpu.VMEM)
    anywhere = pl.BlockSpec(memory_space=pl.ANY)
    sizes = (n, nh, rows, kvh, groups, doc_lengths.shape[0], subs)
    return pl.pallas_call(
        functools.partial(kernel, sizes),
        out_shape=(
            jax.ShapeDtypeStruct((1, rows, feats), f32),
            jax.ShapeDtypeStruct((rows, kc), f32),
            jax.ShapeDtypeStruct((rows, kc), f32),
        ),
        in_specs=[anywhere, full, full, anywhere, full, anywhere, pl.BlockSpec(memory_space=pltpu.SMEM)],
        out_specs=(full, full, full),
        scratch_shapes=[
            vmem((2 * ys * subs, width, sw), bf),
            vmem((rows, feats), bf),
            vmem((rows, feats), bf),
            vmem((n, rows, kc), bf),
            vmem((n, rows, kc), bf),
            vmem((ys * subs, rows, sw), f32),
            vmem((ys * subs, rows, sw), f32),
            vmem((others, rows, sw), bf),
            vmem((others, rows, sw), bf),
            vmem((subs, rows, sw), f32),
            vmem((kvh, stack, HD), bf),
            vmem((kvh, stack, HD), bf),
            vmem((kvh, n, rows, stack), f32),
            vmem((n, rows, rows), f32),
            vmem((kvh, 8, stack), f32),
            vmem((kvh, 8, stack), f32),
            vmem((rows, stack), bf),
            vmem((rows, stack), bf),
            vmem((HD, stack), f32),
            vmem((kvh, n, rows, HD), bf),
            vmem((kvh, n, rows, HD), bf),
            vmem((kvh, n, rows, HD), f32),
            vmem((kvh, n, rows, HD), bf),
            vmem((kvh, n, rows, HD), bf),
            vmem((rows, kc), f32),
            vmem((rows, kc), f32),
            dma((2 * ys * subs,)),
            dma((2,)),
            dma((2, n)), dma((2, n)), dma((2, n)), dma((2, n)),
            dma((ys * subs,)), dma((ys * subs,)),
            dma((others,)), dma((others,)),
            dma((kvh, n)), dma((kvh, n)), dma((kvh, n)), dma((kvh, n)),
            dma(()), dma(()),
        ],
        compiler_params=pltpu.CompilerParams(
            collective_id=0, has_side_effects=True, vmem_limit_bytes=60 * 2**20
        ),
        name="fused",
    )(query, key_cache, value_cache, saved_output, out_grad, out_weight[0], doc_lengths)


def solution(mesh):
    placed = (
        P("phase", "ctx", "head"),
        P("ctx", "head"),
        P("ctx", "head"),
        P("phase", "ctx", "head"),
        P("phase", "ctx", "head"),
        P("phase", "head", None),
        P(),
    )
    return jax.shard_map(
        functools.partial(body, mesh.shape["ctx"], mesh.shape["head"]),
        mesh=mesh,
        in_specs=placed,
        out_specs=(P("phase", "ctx", "head"), P("ctx", "head"), P("ctx", "head")),
        check_vma=False,
    )
```

```python
import functools
import math

import jax
import jax.numpy as jnp
from jax import lax
from jax.experimental import pallas as pl
from jax.experimental.pallas import tpu as pltpu
from jax.sharding import PartitionSpec as P

HD = 128
MASKED = -1e30
LAG = 2
AHEAD = 4
MESH = pl.DeviceIdType.MESH


def nt(a, b):
    return lax.dot_general(a, b, (((1,), (1,)), ((), ())), preferred_element_type=jnp.float32)


def nn(a, b):
    return jnp.dot(a, b, preferred_element_type=jnp.float32)


def kernel(
    sizes,
    query_ref, key_ref, value_ref, saved_ref, grad_ref, weight_ref, doc_ref,
    dq_ref, dk_ref, dv_ref,
    wbuf, qbuf, obuf, kall, vall, psend, precv, ysend, yrecv, own, qs, gs, prob, bias, inv, delta,
    plow, dlow, dqt, xsend, xrecv, keep, zsend, zrecv, fsend, frecv,
    w_sem, in_sem, kv_s, kv_r, fw_s, fw_r, p_s, p_r, y_s, y_r, x_s, x_r, z_s, z_r, f_s, f_r,
):
    n, nh, rows, kvh, groups, docs, subs = sizes
    ys = nh // 2
    feats = kvh * groups * HD
    sw = feats // subs
    half = rows // 2
    scale = HD ** (-0.5)
    phase = lax.axis_index("phase")
    rank = lax.axis_index("ctx")
    head = lax.axis_index("head")
    y, core = head // 2, lax.rem(head, 2)
    other = 1 - phase
    partner = head + 1 - 2 * core
    mine = pl.ds(pl.multiple_of(phase * half, half), half)

    count = ys * subs

    def load(which, q):
        dest = lax.rem(y + q // subs + 1, ys) * 2 + (1 - core if which == 0 else core)
        at = pl.multiple_of(dest * feats + lax.rem(q, subs) * sw, HD)
        i = which * count + q
        return pltpu.make_async_copy(weight_ref.at[:, pl.ds(at, sw)], wbuf.at[i], w_sem.at[i])

    for t in range(AHEAD):
        if t < count:
            load(0, jnp.int32(t)).start()
        if 0 <= t - LAG < count:
            load(1, jnp.int32(t - LAG)).start()
    query_copy = pltpu.make_async_copy(query_ref.at[0], qbuf, in_sem.at[0])
    saved_copy = pltpu.make_async_copy(saved_ref.at[0], obuf, in_sem.at[1])

    barrier = pltpu.get_barrier_semaphore()
    pl.semaphore_signal(barrier, inc=1, device_id={"phase": other}, device_id_type=MESH)
    pl.semaphore_signal(barrier, inc=1, device_id={"head": partner}, device_id_type=MESH)
    for dy in range(1, ys):
        there = lax.rem(y + dy, ys) * 2 + core
        pl.semaphore_signal(barrier, inc=1, device_id={"head": there}, device_id_type=MESH)
    for d in range(1, n):
        pl.semaphore_signal(barrier, inc=1, device_id={"ctx": lax.rem(rank + d, n)}, device_id_type=MESH)
    pl.semaphore_wait(barrier, 2 + (ys - 1) + (n - 1))

    def kv_copy(which, d):
        src, dst = ((key_ref, kall), (value_ref, vall))[which]
        return pltpu.make_async_remote_copy(
            src_ref=src.at[mine], dst_ref=dst.at[rank, mine],
            send_sem=kv_s.at[which, d], recv_sem=kv_r.at[which, d],
            device_id={"ctx": rank + d}, device_id_type=MESH,
        )

    def kv_arrival(which, d):
        dst = (kall, vall)[which].at[rank - d, mine]
        return pltpu.make_async_remote_copy(
            src_ref=dst, dst_ref=dst,
            send_sem=fw_s.at[which, d], recv_sem=kv_r.at[which, d],
            device_id={"phase": other}, device_id_type=MESH,
        )

    def forward(which, d):
        dst = (kall, vall)[which].at[rank - d, mine]
        return pltpu.make_async_remote_copy(
            src_ref=dst, dst_ref=dst,
            send_sem=fw_s.at[which, d], recv_sem=fw_r.at[which, d],
            device_id={"phase": other}, device_id_type=MESH,
        )

    for which in range(2):
        @pl.loop(1, n - rank)
        def _(d):
            kv_copy(which, d).start()

    kall[rank] = key_ref[...]
    vall[rank] = value_ref[...]

    def to_partner(q):
        return pltpu.make_async_remote_copy(
            src_ref=psend.at[q], dst_ref=precv.at[q], send_sem=p_s.at[q], recv_sem=p_r.at[q],
            device_id={"head": partner}, device_id_type=MESH,
        )

    def to_chip(q):
        return pltpu.make_async_remote_copy(
            src_ref=ysend.at[q], dst_ref=yrecv.at[q], send_sem=y_s.at[q], recv_sem=y_r.at[q],
            device_id={"head": lax.rem(y + q // subs + 1, ys) * 2 + core}, device_id_type=MESH,
        )

    far = (ys - 1) * subs

    @pl.loop(0, count + LAG)
    def _(t):
        @pl.when(t + AHEAD < count)
        def _():
            load(0, t + AHEAD).start()

        @pl.when(t + AHEAD - LAG < count)
        def _():
            load(1, t + AHEAD - LAG).start()

        @pl.when(t < count)
        def _():
            load(0, t).wait()
            psend[t] = nn(grad_ref[0], wbuf[t])
            to_partner(t).start()

        @pl.when(t >= LAG)
        def _():
            q = t - LAG
            load(1, q).wait()
            part = nn(grad_ref[0], wbuf[count + q])
            to_partner(q).wait_recv()
            part = part + precv[q]

            @pl.when(q < far)
            def _():
                ysend[q] = part.astype(jnp.bfloat16)
                to_chip(q).start()

            @pl.when(q >= far)
            def _():
                own[q - far] = part

        @pl.when(t == count - AHEAD)
        def _():
            query_copy.start()
            saved_copy.start()

    query_copy.wait()
    @pl.loop(0, kvh * groups)
    def _(h):
        span = pl.ds(pl.multiple_of(lax.rem(h, groups) * rows, rows), rows)
        qs[h // groups, span] = qbuf[:, pl.ds(pl.multiple_of(h * HD, HD), HD)]

    query_place = rank * rows + lax.broadcasted_iota(jnp.int32, (1, rows), 1)
    begin = jnp.zeros((1, rows), jnp.int32)
    end = jnp.int32(0)
    for d in range(docs):
        end = end + doc_ref[d]
        begin = jnp.where(query_place >= end, jnp.maximum(begin, end), begin)

    @pl.loop(0, rank + 1)
    def _(b):
        place = b * rows + lax.broadcasted_iota(jnp.int32, (rows, rows), 0)
        bias[b] = jnp.where((place <= query_place) & (place >= begin), 0.0, MASKED)

    @pl.loop(1, rank + 1)
    def _(d):
        kv_arrival(0, d).wait_recv()
        forward(0, d).start()

    @pl.loop(1, rank + 1)
    def _(d):
        kv_arrival(1, d).wait_recv()
        forward(1, d).start()

    def forwarded(which, d):
        dst = (kall, vall)[which].at[rank - d, pl.ds(pl.multiple_of(other * half, half), half)]
        return pltpu.make_async_remote_copy(
            src_ref=dst, dst_ref=dst, send_sem=fw_s.at[which, d], recv_sem=fw_r.at[which, d],
            device_id={"phase": other}, device_id_type=MESH,
        )

    @pl.loop(1, rank + 1)
    def _(d):
        forwarded(0, d).wait_recv()

    factor = scale * math.log2(math.e)
    @pl.loop(0, kvh)
    def _(j):
        cols = pl.ds(pl.multiple_of(j * HD, HD), HD)

        def score_step(b, largest):
            raised = []
            keys = kall[b, :, cols]
            for g in range(groups):
                span = slice(g * rows, (g + 1) * rows)
                s = nt(keys, qs[j, span]) * factor + bias[b]
                prob[j, b, :, span] = s
                raised.append(jnp.maximum(largest[g], jnp.max(s, axis=0, keepdims=True)))
            return tuple(raised)

        largest = lax.fori_loop(
            0, rank + 1, score_step, (jnp.full((1, rows), MASKED, jnp.float32),) * groups
        )

        def exp_step(b, total):
            sums = []
            for g in range(groups):
                span = slice(g * rows, (g + 1) * rows)
                e = jnp.exp2(prob[j, b, :, span] - largest[g])
                prob[j, b, :, span] = e
                sums.append(total[g] + jnp.sum(e, axis=0, keepdims=True))
            return tuple(sums)

        total = lax.fori_loop(
            0, rank + 1, exp_step, (jnp.zeros((1, rows), jnp.float32),) * groups
        )
        for g in range(groups):
            inv[j, :, g * rows:(g + 1) * rows] = jnp.broadcast_to(1.0 / total[g], (8, rows))

    saved_copy.wait()
    ones = jnp.ones((8, HD), jnp.bfloat16)
    @pl.loop(0, subs)
    def _(s):
        part = own[s]
        for dy in range(1, ys):
            to_chip((dy - 1) * subs + s).wait_recv()
            part = part + yrecv[(dy - 1) * subs + s].astype(jnp.float32)
        low = part.astype(jnp.bfloat16)
        for a in range(sw // HD):
            h = s * (sw // HD) + a
            span = pl.ds(pl.multiple_of(lax.rem(h, groups) * rows, rows), rows)
            one = low[:, a * HD:(a + 1) * HD]
            gs[h // groups, span] = one
            saved = obuf[:, pl.ds(pl.multiple_of(h * HD, HD), HD)]
            both = one.astype(jnp.float32) * saved.astype(jnp.float32)
            high = both.astype(jnp.bfloat16)
            rest = (both - high.astype(jnp.float32)).astype(jnp.bfloat16)
            delta[h // groups, :, span] = nt(ones, high) + nt(ones, rest)

    @pl.loop(1, rank + 1)
    def _(d):
        forwarded(1, d).wait_recv()

    def to_phase(j, b):
        return pltpu.make_async_remote_copy(
            src_ref=xsend.at[j, b], dst_ref=xrecv.at[j, b], send_sem=x_s.at[j, b], recv_sem=x_r.at[j, b],
            device_id={"phase": other}, device_id_type=MESH,
        )

    def to_owner(j, b):
        return pltpu.make_async_remote_copy(
            src_ref=zsend.at[j, b], dst_ref=zrecv.at[j, rank - b],
            send_sem=z_s.at[j, rank - b], recv_sem=z_r.at[j, rank - b],
            device_id={"ctx": b}, device_id_type=MESH,
        )

    def from_later(j, d):
        return pltpu.make_async_remote_copy(
            src_ref=zsend.at[j, 0], dst_ref=zrecv.at[j, d], send_sem=z_s.at[j, d], recv_sem=z_r.at[j, d],
            device_id={"ctx": lax.rem(rank + d, n)}, device_id_type=MESH,
        )

    def send_on(j, b):
        to_phase(j, b).wait_recv()
        zsend[j, b] = (keep[j, b] + xrecv[j, b].astype(jnp.float32)).astype(jnp.bfloat16)
        to_owner(j, b).start()

    @pl.loop(0, kvh)
    def _(j):
        cols = pl.ds(pl.multiple_of(j * HD, HD), HD)
        dqt[...] = jnp.zeros_like(dqt)

        @pl.loop(0, rank + 1)
        def _(b):
            values = vall[b, :, cols]
            for g in range(groups):
                span = slice(g * rows, (g + 1) * rows)
                p = prob[j, b, :, span] * inv[j, 0:1, span]
                plow[:, span] = p.astype(jnp.bfloat16)
                wide = nt(values, gs[j, span])
                dlow[:, span] = (p * (wide - delta[j, 0:1, span])).astype(jnp.bfloat16)
            dv = nn(plow[...], gs[j])
            dk = nn(dlow[...], qs[j]) * scale
            keep[j, b] = jnp.where(phase == 0, dk, dv)
            xsend[j, b] = jnp.where(phase == 0, dv, dk).astype(jnp.bfloat16)
            to_phase(j, b).start()
            turned = kall[b, :, cols].astype(jnp.float32).T.astype(jnp.bfloat16)
            dqt[...] += nn(turned, dlow[...])

            @pl.when((j > 0) & (b < rank))
            def _():
                send_on(j - 1, b)

        for g in range(groups):
            at = pl.ds(pl.multiple_of((j * groups + g) * HD, HD), HD)
            dq_ref[0, :, at] = dqt[:, g * rows:(g + 1) * rows].T * scale

    @pl.loop(0, rank)
    def _(b):
        send_on(kvh - 1, b)

    def last(j):
        return pltpu.make_async_remote_copy(
            src_ref=fsend.at[j], dst_ref=frecv.at[j], send_sem=f_s.at[j], recv_sem=f_r.at[j],
            device_id={"phase": other}, device_id_type=MESH,
        )

    @pl.loop(0, kvh)
    def _(j):
        to_phase(j, rank).wait_recv()
        fsend[j] = keep[j, rank] + xrecv[j, rank].astype(jnp.float32)

        @pl.loop(1, n - rank)
        def _(d):
            from_later(j, d).wait_recv()
            fsend[j] += zrecv[j, d].astype(jnp.float32)

        last(j).start()

    for which in range(2):
        @pl.loop(1, n - rank)
        def _(d):
            kv_copy(which, d).wait_send()

        @pl.loop(1, rank + 1)
        def _(d):
            forward(which, d).wait_send()

    @pl.loop(0, count)
    def _(q):
        to_partner(q).wait_send()

    @pl.loop(0, far)
    def _(q):
        to_chip(q).wait_send()

    @pl.loop(0, kvh)
    def _(j):
        @pl.loop(0, rank + 1)
        def _(b):
            to_phase(j, b).wait_send()

        @pl.loop(0, rank)
        def _(b):
            to_owner(j, b).wait_send()

    for j in range(kvh):
        last(j).wait()
        cols = slice(j * HD, (j + 1) * HD)
        dk_ref[:, cols] = jnp.where(phase == 0, fsend[j], frecv[j])
        dv_ref[:, cols] = jnp.where(phase == 0, frecv[j], fsend[j])


def body(n, nh, query, key_cache, value_cache, saved_output, out_grad, out_weight, doc_lengths):
    rows, feats = query.shape[1:]
    width, kc = out_weight.shape[1], key_cache.shape[1]
    kvh = kc // HD
    groups = feats // kc
    ys, subs = nh // 2, groups
    sw = feats // subs
    bf, f32 = jnp.bfloat16, jnp.float32
    vmem = pltpu.VMEM
    dma = pltpu.SemaphoreType.DMA
    others = max(ys - 1, 1) * subs
    stack = groups * rows
    full = pl.BlockSpec(memory_space=pltpu.VMEM)
    anywhere = pl.BlockSpec(memory_space=pl.ANY)
    sizes = (n, nh, rows, kvh, groups, doc_lengths.shape[0], subs)
    results = pl.pallas_call(
        functools.partial(kernel, sizes),
        out_shape=(
            jax.ShapeDtypeStruct((1, rows, feats), f32),
            jax.ShapeDtypeStruct((rows, kc), f32),
            jax.ShapeDtypeStruct((rows, kc), f32),
        ),
        in_specs=[anywhere, full, full, anywhere, full, anywhere, pl.BlockSpec(memory_space=pltpu.SMEM)],
        out_specs=(full, full, full),
        scratch_shapes=[
            vmem((2 * ys * subs, width, sw), bf),
            vmem((rows, feats), bf),
            vmem((rows, feats), bf),
            vmem((n, rows, kc), bf),
            vmem((n, rows, kc), bf),
            vmem((ys * subs, rows, sw), f32),
            vmem((ys * subs, rows, sw), f32),
            vmem((others, rows, sw), bf),
            vmem((others, rows, sw), bf),
            vmem((subs, rows, sw), f32),
            vmem((kvh, stack, HD), bf),
            vmem((kvh, stack, HD), bf),
            vmem((kvh, n, rows, stack), f32),
            vmem((n, rows, rows), f32),
            vmem((kvh, 8, stack), f32),
            vmem((kvh, 8, stack), f32),
            vmem((rows, stack), bf),
            vmem((rows, stack), bf),
            vmem((HD, stack), f32),
            vmem((kvh, n, rows, HD), bf),
            vmem((kvh, n, rows, HD), bf),
            vmem((kvh, n, rows, HD), f32),
            vmem((kvh, n, rows, HD), bf),
            vmem((kvh, n, rows, HD), bf),
            vmem((kvh, rows, HD), f32),
            vmem((kvh, rows, HD), f32),
            dma((2 * ys * subs,)),
            dma((2,)),
            dma((2, n)), dma((2, n)), dma((2, n)), dma((2, n)),
            dma((ys * subs,)), dma((ys * subs,)),
            dma((others,)), dma((others,)),
            dma((kvh, n)), dma((kvh, n)), dma((kvh, n)), dma((kvh, n)),
            dma((kvh,)), dma((kvh,)),
        ],
        compiler_params=pltpu.CompilerParams(
            collective_id=0, has_side_effects=True, vmem_limit_bytes=60 * 2**20
        ),
        name="fused",
    )(query, key_cache, value_cache, saved_output, out_grad, out_weight[0], doc_lengths)
    return results


def solution(mesh):
    placed = (
        P("phase", "ctx", "head"),
        P("ctx", "head"),
        P("ctx", "head"),
        P("phase", "ctx", "head"),
        P("phase", "ctx", "head"),
        P("phase", "head", None),
        P(),
    )
    return jax.shard_map(
        functools.partial(body, mesh.shape["ctx"], mesh.shape["head"]),
        mesh=mesh,
        in_specs=placed,
        out_specs=(P("phase", "ctx", "head"), P("ctx", "head"), P("ctx", "head")),
        check_vma=False,
    )
```
